512 devices in a mesh: dp: 32 (over y_lo, x, core), fsdp: 16 (over y_hi, z).
Axes of the slice: x: 4, y: 8 (y_hi: 2, y_lo: 4; y = y_hi * 4 + y_lo), z: 8, core: 2. Of those that a mesh axis runs over, the one named last changes fastest.
Arguments:
- partials: bfloat16 [32, 16, 2, 512, 512], P('dp', 'fsdp'), may hold values from -16 to 32, as said below
- basis_store: bfloat16 [32, 16, 2, 512, 512], P('dp', 'fsdp'), may hold values from -1 to 2
- owner_table: int32 [16], replicated, may hold values from 1 to 31, as said below
- grad: bfloat16 [16, 512, 512], P('fsdp', 'dp'), may hold values from -6 to 6
- exp_avg: float32 [16, 512, 512], P('fsdp', 'dp'), may hold values from -2 to 2
- exp_avg_sq: float32 [16, 512, 512], P('fsdp', 'dp'), may hold values from 0.25 to 4
Outputs:
- basis_new: bfloat16 [16, 2, 512, 512], P('fsdp')
- exp_avg_new: float32 [16, 512, 512], P('fsdp', 'dp')
- exp_avg_sq_new: float32 [16, 512, 512], P('fsdp', 'dp')
- update: bfloat16 [16, 512, 512], P('fsdp', 'dp')
The draws below stay inside these ranges and needn't reach their ends.
Inputs may be any that keep to these rules, and one draw needn't show every extreme that they name: `partials`: for every block and factor the sum over the 32 replicas is symmetric and positive definite. `owner_table`: distinct data indices, 2 apart in a rotated order, the largest 32 - 1.
All inputs are finite; a program needn't handle non-finite values.
Results may differ from the reference program's by a relative error of at most 0.014.
Values may be sent and summed in bfloat16 or wider, within the bound.
No kernel may reach another device: no remote copies, remote signals or barrier semaphores. Data moves between devices by JAX's collectives and lax.ppermute only.
A program may use at most 64 MiB of HBM per device.

```python
import math
import jax
import jax.numpy as jnp
from jax import lax

BLK = 512
STEPS = 2
BLOCKS = 16
N_DP = 32


def draw_partials(key, part):
    key = jax.random.fold_in(key, 11)
    key_scale, key_gain, key_noise = jax.random.split(key, 3)
    scales = jnp.exp(jax.random.uniform(key_scale, (BLOCKS, 2, BLK), jnp.float32, 0.0, math.log(10.0)))
    gains = jax.random.uniform(key_gain, (N_DP, BLOCKS, 2, BLK), jnp.float32, 0.5, 1.5)
    noise = jax.random.truncated_normal(key_noise, -4.0, 4.0, (N_DP, BLOCKS, 2, BLK, BLK), jnp.float32)
    symmetric = (noise + jnp.swapaxes(noise, -1, -2)) * (1.0 / math.sqrt(2.0))
    roots = jnp.sqrt(scales)
    spread = roots[None, :, :, :, None] * roots[None, :, :, None, :]
    identity = jnp.eye(BLK, dtype=jnp.float32)
    off_diagonal = 1.2 * symmetric * spread * (1.0 / math.sqrt(BLK)) * (1.0 - identity)
    diagonal = (gains * scales[None])[..., None] * identity
    return (off_diagonal + diagonal).astype(jnp.bfloat16)


def draw_basis_store(key, part):
    key = jax.random.fold_in(key, 37)
    shape = (N_DP, BLOCKS, 2, BLK, BLK)
    noise = jax.random.truncated_normal(key, -4.0, 4.0, shape, jnp.float32)
    identity = jnp.eye(BLK, dtype=jnp.float32)
    return (identity + 0.2 * noise * (1.0 / math.sqrt(BLK))).astype(jnp.bfloat16)


def draw_owner_table(key, part):
    key = jax.random.fold_in(key, 23)
    rotation = jax.random.randint(key, (), 0, BLOCKS, jnp.int32)
    spacing = N_DP // BLOCKS
    order = (jnp.arange(BLOCKS, dtype=jnp.int32) + rotation) % BLOCKS
    return (N_DP - 1 - order * spacing).astype(jnp.int32)


def level_of(rng, extent, shards, smallest, top_value):
    def one(axis_at, parts):
        heights = jax.random.uniform(jax.random.fold_in(jax.random.fold_in(rng, 6), axis_at), (parts,), jnp.float32, smallest / len(shards), top_value / len(shards))
        return jnp.repeat(jnp.exp(heights), extent[axis_at] // parts).reshape((-1,) + (1,) * (len(extent) - axis_at - 1))

    factor_of = one(*shards[0])
    for cut in shards[1:]:
        factor_of = factor_of * one(*cut)
    return factor_of


def bell_draw(key, dims, width, reach, cuts=(), held_as=jnp.bfloat16):
    gain = level_of(key, dims, cuts, -0.22, 0.18) if cuts else 1.0
    result = jax.random.normal(key, dims, jnp.float32) * width * gain
    return jnp.minimum(jnp.maximum(result, -reach), reach).astype(held_as)


def setup_inputs(seed: int = 0) -> dict:
    streams_of = jax.random.split(jax.random.key(seed), 7)
    return {
        "partials": draw_partials(jax.random.fold_in(streams_of[6], 71), 0),
        "basis_store": draw_basis_store(jax.random.fold_in(streams_of[6], 71), 0),
        "owner_table": draw_owner_table(jax.random.fold_in(streams_of[6], 71), 0),
        "grad": bell_draw(streams_of[3], (BLOCKS, BLK, BLK), 1.0, 6.0, ((0, 16), (1, 32))),
        "exp_avg": bell_draw(streams_of[4], (BLOCKS, BLK, BLK), 0.3, 2.0, ((0, 16), (1, 32)), jnp.float32),
        "exp_avg_sq": jnp.clip(jnp.exp(math.log(4.0) - 2.7725887 * jax.random.uniform(streams_of[5], (BLOCKS, BLK, BLK), jnp.float32) ** level_of(streams_of[5], (BLOCKS, BLK, BLK), ((0, 16), (1, 32)), -0.2, 0.2)), 0.25, 4.0),
    }


FULL = lax.Precision.HIGHEST

def orthonormal_step(factor, initial):
    images = jnp.dot(factor.astype(jnp.float32), initial.astype(jnp.float32), precision=FULL, preferred_element_type=jnp.float32)
    gram_matrix = jnp.dot(images.T.astype(jnp.float32), images.astype(jnp.float32), precision=FULL, preferred_element_type=jnp.float32)
    lower_factor = jnp.linalg.cholesky(gram_matrix)
    return lax.linalg.triangular_solve(lower_factor, images, left_side=False, lower=True, transpose_a=True)

def reference(partials, basis_store, owner_table, grad, exp_avg, exp_avg_sq):
    factors = lax.optimization_barrier(jnp.sum(partials, axis=0, dtype=jnp.float32))
    previous = basis_store[owner_table, jnp.arange(BLOCKS, dtype=jnp.int32)]
    current = previous.astype(jnp.float32)
    for repeat in range(STEPS):
        current = jax.vmap(jax.vmap(orthonormal_step))(factors, current)
    fresh = current.astype(jnp.bfloat16)
    left_new = fresh[:, 0].astype(jnp.float32)
    right_new = fresh[:, 1].astype(jnp.float32)
    left_old = previous[:, 0].astype(jnp.float32)
    right_old = previous[:, 1].astype(jnp.float32)
    projected = jnp.einsum('bij,bjk->bik', grad.astype(jnp.float32), right_new, precision=FULL).astype(jnp.bfloat16)
    gradient_rot = jnp.einsum('bji,bjk->bik', left_new, projected.astype(jnp.float32), precision=FULL)
    left_turn = jnp.einsum('bji,bjk->bik', left_new, left_old, precision=FULL)
    right_turn = jnp.einsum('bji,bjk->bik', right_new, right_old, precision=FULL)
    moment_back = jnp.einsum('bij,bkj->bik', exp_avg, right_turn, precision=FULL)
    moment_rot = jnp.einsum('bij,bjk->bik', left_turn, moment_back, precision=FULL)
    moment_new = 0.9 * moment_rot + 0.1 * gradient_rot
    square_new = 0.95 * exp_avg_sq + 0.05 * gradient_rot * gradient_rot
    direction = (moment_new / (jnp.sqrt(square_new) + 1e-08)).astype(jnp.bfloat16)
    returned = jnp.einsum('bij,bkj->bik', direction.astype(jnp.float32), right_new, precision=FULL).astype(jnp.bfloat16)
    update = jnp.einsum('bij,bjk->bik', left_new, returned.astype(jnp.float32), precision=FULL).astype(jnp.bfloat16)
    return (fresh, moment_new, square_new, update)
```

```python
import functools

import jax
import jax.numpy as jnp
from jax import lax
from jax.experimental import pallas as pl
from jax.experimental.pallas import tpu as pltpu
from jax.sharding import PartitionSpec as P

F32 = jnp.float32
BF16 = jnp.bfloat16
FULL = lax.Precision.HIGHEST
B = 128
N = 512
NB = N // B
CHIPS = 16
UPPER = [(i, j) for i in range(NB) for j in range(i, NB)]
PACK = len(UPPER) * B
PF = PACK // CHIPS
PQ = N * NB // CHIPS
PIECE = PF + PQ
STEP = 16
RELAX = (1.4, 1.4, 1.4, 1.4, 1.0, 1.0)
START = 0.6
TOLERANCE = 0.03
PIVOT = 1e-4

PARAMS = pltpu.CompilerParams(vmem_limit_bytes=48 * 1024 * 1024)
SMEM = pl.BlockSpec(memory_space=pltpu.SMEM)
VMEM = pl.BlockSpec(memory_space=pltpu.VMEM)


def spec(i):
    return slice(i * B, (i + 1) * B)


def dot(a, b):
    return jnp.dot(a, b, preferred_element_type=F32)


def dot_tn(a, b):
    return lax.dot_general(a, b, (((0,), (0,)), ((), ())), preferred_element_type=F32)


def dot_nt(a, b):
    return lax.dot_general(a, b, (((1,), (1,)), ((), ())), preferred_element_type=F32)


def split(x):
    high = x.astype(BF16)
    return high, (x - high.astype(F32)).astype(BF16)


def dot3(a, b, op=dot):
    ah, al = a
    bh, bl = b
    return op(ah, bh) + (op(ah, bl) + op(al, bh))


def pieces(t):
    row, end = t * B, (t + 1) * B
    while row < end:
        piece = row // PF
        count = min(end, (piece + 1) * PF) - row
        yield piece, row - piece * PF, row - t * B, count
        row += count


def pack_kernel(meta, part, out):
    other = 1 - meta[0]
    for t, (i, j) in enumerate(UPPER):
        out[t * B : (t + 1) * B, :] = part[other, spec(i), spec(j)]


def pair_kernel(meta, part, got, got_basis, basis, out):
    core = meta[0]
    for t, (i, j) in enumerate(UPPER):
        total = part[core, spec(i), spec(j)].astype(F32) + got[t * B : (t + 1) * B, :].astype(F32)
        total = total.astype(BF16)
        for piece, at, row, count in pieces(t):
            out[piece, at : at + count, :] = total[row : row + count]

    @pl.when(core == 0)
    def _():
        for k in range(CHIPS):
            out[k, PF:, :] = got_basis[spec(k % NB), spec(k // NB)]

    @pl.when(core == 1)
    def _():
        for k in range(CHIPS):
            out[k, PF:, :] = basis[1, spec(k % NB), spec(k // NB)]


def sum_kernel(meta, got, out):
    owner = meta[2]
    total = got[0, :PF, :].astype(F32)
    for k in range(1, CHIPS):
        total = total + got[k, :PF, :].astype(F32)
    total = total.astype(BF16)
    chosen = got[owner, PF:, :]
    for k in range(CHIPS):
        out[k, :PF, :] = total
        out[k, PF:, :] = chosen


def unpack_basis(got, out):
    for k in range(CHIPS):
        out[spec(k % NB), spec(k // NB)] = got[k, PF:, :]


def grid_of(n):
    return (
        lax.broadcasted_iota(jnp.int32, (n, n), 0),
        lax.broadcasted_iota(jnp.int32, (n, n), 1),
    )


def eliminate(gram, current):
    lane = lax.broadcasted_iota(jnp.int32, (1, N), 1)
    sub = lax.broadcasted_iota(jnp.int32, (N, 1), 0)

    def step(j, carry):
        row = gram[pl.ds(j, 1), :]
        pivot = jnp.sum(jnp.where(lane == j, row, 0.0), axis=1, keepdims=True)
        ratio = jnp.where(lane > j, row / pivot, 0.0)
        g = gram[...]
        column = jnp.sum(jnp.where(lane == j, g, 0.0), axis=1, keepdims=True)
        gram[...] = g - jnp.where(sub > j, column, 0.0) * ratio
        a = current[...]
        column = jnp.sum(jnp.where(lane == j, a, 0.0), axis=1, keepdims=True)
        current[...] = jnp.where(lane == j, a * lax.rsqrt(pivot), a - column * ratio)
        return carry

    lax.fori_loop(0, N, step, 0)


def basis_kernel(got, out, factor, start, packed, gram, images):
    for k in range(CHIPS):
        packed[k * PF : (k + 1) * PF, :] = got[k, :PF, :]
    for t, (i, j) in enumerate(UPPER):
        block = packed[t * B : (t + 1) * B, :]
        factor[spec(i), spec(j)] = block
        if i != j:
            factor[spec(j), spec(i)] = block.T
    unpack_basis(got, start)

    f = factor[...]
    ah, al = split(dot(f, start[...]))
    t = dot(f, ah) + dot(f, al)
    images[...] = t
    th, tl = split(t)
    gram[...] = dot3((th, tl), (th, tl), dot_tn)

    rows, cols = grid_of(B)
    eye = rows == cols
    unit = jnp.where(eye, 1.0, 0.0)
    lengths = jnp.sum(t * t, axis=0, keepdims=True)
    fault = jnp.zeros((B, B), F32)
    for k in range(NB):
        h = gram[spec(k), spec(k)]
        on = jnp.where(eye, h, 0.0)
        pivots = jnp.sum(on, axis=0, keepdims=True)
        fault = jnp.where(pivots > PIVOT * lengths[:, spec(k)], fault, 1.0)
        down = lax.rsqrt(jnp.sum(on, axis=1, keepdims=True)) * START
        across = lax.rsqrt(pivots) * START
        h = h * down * across
        p = None
        for step, relax in enumerate(RELAX):
            e = h - unit
            weights = jnp.where(eye, 0.5 * relax, relax)
            upper = unit - jnp.where(rows <= cols, e * weights, 0.0)
            us = split(upper)
            if step < len(RELAX) - 1:
                lower = unit - jnp.where(rows >= cols, e * weights, 0.0)
                hu = dot3(split(h), us)
                h = dot3(split(lower), split(hu))
            else:
                fault = jnp.where(jnp.abs(e) < TOLERANCE, fault, 1.0)
            p = upper if p is None else dot3(split(p), us)
        s = p * down
        ss = split(s)
        q = dot3(split(images[:, spec(k)]), ss)
        out[:, spec(k)] = q.astype(BF16)
        if k < NB - 1:
            rest = slice((k + 1) * B, N)
            r = dot3(split(s.T), split(gram[spec(k), rest]))
            rs = split(r)
            gram[rest, rest] = gram[rest, rest] - dot3(rs, rs, dot_tn)
            images[:, rest] = images[:, rest] - dot3(split(q), rs)

    @pl.when(jnp.max(fault) > 0.0)
    def _():
        images[...] = start[...].astype(F32)
        for repeat in range(2):
            image = jnp.dot(
                factor[...].astype(F32), images[...], precision=FULL, preferred_element_type=F32
            )
            images[...] = image
            gram[...] = lax.dot_general(
                image, image, (((0,), (0,)), ((), ())), precision=FULL, preferred_element_type=F32
            )
            eliminate(gram, images)
        out[...] = images[...].astype(BF16)


def turn_kernel(meta, mine, theirs, rows, out, bases):
    core = meta[0]
    for k in range(CHIPS):
        bases[core, spec(k % NB), spec(k // NB)] = mine[k, PF:, :]
        bases[1 - core, spec(k % NB), spec(k // NB)] = theirs[k, PF:, :]
    moment = rows[:, STEP : 2 * STEP, :].reshape(N, N)
    half = dot(bases[0], moment).astype(BF16)
    out[...] = dot_nt(half, bases[1]).astype(BF16)


def final_kernel(meta, mine, theirs, turned, rows, square, fresh, moment_out, square_out, update, mom, rot):
    core = meta[0]
    fresh[core] = mine[...]
    fresh[1 - core] = theirs[...]
    left = fresh[0]
    right = fresh[1]
    grad = rows[:, :STEP, :].reshape(N, N)
    projected = dot(grad, right).astype(BF16)
    moment = dot(turned[...], right).astype(BF16)
    gradient_rot = dot_tn(left, projected)
    moment_rot = dot_tn(left, moment)
    new = 0.9 * moment_rot + 0.1 * gradient_rot
    mom[...] = new
    rot[...] = gradient_rot
    squares = rows[:, 2 * STEP :, :].reshape(N, N).astype(F32)
    level = 0.95 * squares + 0.05 * gradient_rot * gradient_rot
    direction = (new / (jnp.sqrt(level) + 1e-08)).astype(BF16)
    returned = dot_nt(direction, right).astype(BF16)
    at = pl.ds(pl.multiple_of(meta[1] * STEP, STEP), STEP)
    moment_out[...] = mom[at, :]
    own = rot[at, :]
    square_out[...] = 0.95 * square[...] + 0.05 * own * own
    update[...] = dot(fresh[0, at, :], returned).astype(BF16)


def shape(dims, dtype):
    return jax.ShapeDtypeStruct(dims, dtype)


def call(kernel, name, out, specs, scratch=(), flops=0):
    return pl.pallas_call(
        kernel,
        name=name,
        out_shape=out,
        in_specs=specs,
        scratch_shapes=list(scratch),
        compiler_params=PARAMS,
        cost_estimate=pl.CostEstimate(flops=flops, bytes_accessed=2**21, transcendentals=0),
    )


def on_device(partials, basis_store, owner_table, grad, exp_avg, exp_avg_sq):
    column = lax.axis_index("fsdp")
    replica = lax.axis_index("dp")
    positions = jnp.arange(owner_table.shape[0], dtype=jnp.int32)
    owner = jnp.sum(jnp.where(positions == column, owner_table, 0))
    core = replica % 2
    meta = jnp.stack([core, replica, owner // 2]).astype(jnp.int32)
    devices = 2 * CHIPS
    swap = [(i, i ^ 1) for i in range(devices)]
    down = [(i, i - 1) for i in range(1, devices, 2)]
    groups = [list(range(c, devices, 2)) for c in range(2)]

    rows = jnp.concatenate([grad[0], exp_avg[0].astype(BF16), exp_avg_sq[0].astype(BF16)], axis=0)
    rows = lax.all_gather(rows, "dp", axis=0, tiled=False)

    part = partials[0, 0]
    stored = basis_store[0, 0]
    got_basis = lax.ppermute(stored[0], "dp", down)
    packed = call(pack_kernel, "pack", shape((PACK, B), BF16), [SMEM, VMEM])(meta, part)
    got = lax.ppermute(packed, "dp", swap)
    payload = call(pair_kernel, "pair", shape((CHIPS, PIECE, B), BF16), [SMEM] + [VMEM] * 4)(
        meta, part, got, got_basis, stored
    )
    got = lax.all_to_all(payload, "dp", 0, 0, tiled=True, axis_index_groups=groups)
    payload = call(sum_kernel, "sum", shape((CHIPS, PIECE, B), BF16), [SMEM, VMEM])(meta, got)
    whole = lax.all_to_all(payload, "dp", 0, 0, tiled=True, axis_index_groups=groups)
    whole_other = lax.ppermute(whole, "dp", swap)
    mine = call(
        basis_kernel,
        "basis",
        shape((N, N), BF16),
        [VMEM],
        [
            pltpu.VMEM((N, N), BF16),
            pltpu.VMEM((N, N), BF16),
            pltpu.VMEM((PACK, B), BF16),
            pltpu.VMEM((N, N), F32),
            pltpu.VMEM((N, N), F32),
        ],
        flops=2**34,
    )(whole)
    theirs = lax.ppermute(mine, "dp", swap)
    turned = call(
        turn_kernel, "turn", shape((N, N), BF16), [SMEM] + [VMEM] * 3, [pltpu.VMEM((2, N, N), BF16)], flops=2**30
    )(meta, whole, whole_other, rows)
    fresh, moment_new, square_new, update = call(
        final_kernel,
        "final",
        (
            shape((2, N, N), BF16),
            shape((STEP, N), F32),
            shape((STEP, N), F32),
            shape((STEP, N), BF16),
        ),
        [SMEM] + [VMEM] * 5,
        [pltpu.VMEM((N, N), F32), pltpu.VMEM((N, N), F32)],
        flops=2**32,
    )(meta, mine, theirs, turned, rows, exp_avg_sq[0])
    return fresh[None], moment_new[None], square_new[None], update[None]


def solution(mesh):
    in_specs = (
        P("dp", "fsdp", None, None, None),
        P("dp", "fsdp", None, None, None),
        P(),
        P("fsdp", "dp", None),
        P("fsdp", "dp", None),
        P("fsdp", "dp", None),
    )
    out_specs = (
        P("fsdp", None, None, None),
        P("fsdp", "dp", None),
        P("fsdp", "dp", None),
        P("fsdp", "dp", None),
    )
    return jax.shard_map(
        on_device, mesh=mesh, in_specs=in_specs, out_specs=out_specs, check_vma=False
    )
```

```python
import functools

import jax
import jax.numpy as jnp
from jax import lax
from jax.experimental import pallas as pl
from jax.experimental.pallas import tpu as pltpu
from jax.sharding import PartitionSpec as P

F32 = jnp.float32
BF16 = jnp.bfloat16
FULL = lax.Precision.HIGHEST
B = 128
N = 512
NB = N // B
CHIPS = 16
UPPER = [(i, j) for i in range(NB) for j in range(i, NB)]
PACK = len(UPPER) * B
PF = PACK // CHIPS
PQ = N * NB // CHIPS
PIECE = PF + PQ
STEP = 16
RELAX = (1.4, 1.4, 1.4, 1.4, 1.0, 1.0)
START = 0.6
TOLERANCE = 0.03
PIVOT = 1e-4

PARAMS = pltpu.CompilerParams(vmem_limit_bytes=48 * 1024 * 1024)
SMEM = pl.BlockSpec(memory_space=pltpu.SMEM)
VMEM = pl.BlockSpec(memory_space=pltpu.VMEM)


def spec(i):
    return slice(i * B, (i + 1) * B)


def dot(a, b):
    return jnp.dot(a, b, preferred_element_type=F32)


def dot_tn(a, b):
    return lax.dot_general(a, b, (((0,), (0,)), ((), ())), preferred_element_type=F32)


def dot_nt(a, b):
    return lax.dot_general(a, b, (((1,), (1,)), ((), ())), preferred_element_type=F32)


def split(x):
    high = x.astype(BF16)
    return high, (x - high.astype(F32)).astype(BF16)


def dot3(a, b, op=dot):
    ah, al = a
    bh, bl = b
    return op(ah, bh) + (op(ah, bl) + op(al, bh))


def pieces(t):
    row, end = t * B, (t + 1) * B
    while row < end:
        piece = row // PF
        count = min(end, (piece + 1) * PF) - row
        yield piece, row - piece * PF, row - t * B, count
        row += count


def here():
    replica = lax.axis_index("dp")
    return replica, lax.rem(replica, 2)


def pack_kernel(part, out):
    other = 1 - here()[1]
    for t, (i, j) in enumerate(UPPER):
        out[t * B : (t + 1) * B, :] = part[other, spec(i), spec(j)]


def pair_kernel(part, got, got_basis, basis, out):
    core = here()[1]
    for t, (i, j) in enumerate(UPPER):
        total = part[core, spec(i), spec(j)].astype(F32) + got[t * B : (t + 1) * B, :].astype(F32)
        total = total.astype(BF16)
        for piece, at, row, count in pieces(t):
            out[piece, at : at + count, :] = total[row : row + count]

    @pl.when(core == 0)
    def _():
        for k in range(CHIPS):
            out[k, PF:, :] = got_basis[0, spec(k % NB), spec(k // NB)]

    @pl.when(core == 1)
    def _():
        for k in range(CHIPS):
            out[k, PF:, :] = basis[1, spec(k % NB), spec(k // NB)]


def sum_kernel(table, got, out):
    owner = lax.div(table[lax.axis_index("fsdp")], 2)
    total = got[0, :PF, :].astype(F32)
    for k in range(1, CHIPS):
        total = total + got[k, :PF, :].astype(F32)
    total = total.astype(BF16)
    chosen = got[owner, PF:, :]
    for k in range(CHIPS):
        out[k, :PF, :] = total
        out[k, PF:, :] = chosen


def unpack_basis(got, out):
    for k in range(CHIPS):
        out[spec(k % NB), spec(k // NB)] = got[k, PF:, :]


def grid_of(n):
    return (
        lax.broadcasted_iota(jnp.int32, (n, n), 0),
        lax.broadcasted_iota(jnp.int32, (n, n), 1),
    )


def eliminate(gram, current):
    lane = lax.broadcasted_iota(jnp.int32, (1, N), 1)
    sub = lax.broadcasted_iota(jnp.int32, (N, 1), 0)

    def step(j, carry):
        row = gram[pl.ds(j, 1), :]
        pivot = jnp.sum(jnp.where(lane == j, row, 0.0), axis=1, keepdims=True)
        ratio = jnp.where(lane > j, row / pivot, 0.0)
        g = gram[...]
        column = jnp.sum(jnp.where(lane == j, g, 0.0), axis=1, keepdims=True)
        gram[...] = g - jnp.where(sub > j, column, 0.0) * ratio
        a = current[...]
        column = jnp.sum(jnp.where(lane == j, a, 0.0), axis=1, keepdims=True)
        current[...] = jnp.where(lane == j, a * lax.rsqrt(pivot), a - column * ratio)
        return carry

    lax.fori_loop(0, N, step, 0)


def basis_kernel(got, out, factor, start, packed, gram, images):
    for k in range(CHIPS):
        packed[k * PF : (k + 1) * PF, :] = got[k, :PF, :]
    for t, (i, j) in enumerate(UPPER):
        block = packed[t * B : (t + 1) * B, :]
        factor[spec(i), spec(j)] = block
        if i != j:
            factor[spec(j), spec(i)] = block.T
    unpack_basis(got, start)

    f = factor[...]
    ah, al = split(dot(f, start[...]))
    t = dot(f, ah) + dot(f, al)
    images[...] = t
    th, tl = split(t)
    gram[...] = dot3((th, tl), (th, tl), dot_tn)

    rows, cols = grid_of(B)
    eye = rows == cols
    unit = jnp.where(eye, 1.0, 0.0)
    lengths = jnp.sum(t * t, axis=0, keepdims=True)
    fault = jnp.zeros((B, B), F32)
    for k in range(NB):
        h = gram[spec(k), spec(k)]
        on = jnp.where(eye, h, 0.0)
        pivots = jnp.sum(on, axis=0, keepdims=True)
        fault = jnp.where(pivots > PIVOT * lengths[:, spec(k)], fault, 1.0)
        down = lax.rsqrt(jnp.sum(on, axis=1, keepdims=True)) * START
        across = lax.rsqrt(pivots) * START
        h = h * down * across
        p = None
        for step, relax in enumerate(RELAX):
            e = h - unit
            weights = jnp.where(eye, 0.5 * relax, relax)
            upper = unit - jnp.where(rows <= cols, e * weights, 0.0)
            us = split(upper)
            if step < len(RELAX) - 1:
                lower = unit - jnp.where(rows >= cols, e * weights, 0.0)
                hu = dot3(split(h), us)
                h = dot3(split(lower), split(hu))
            else:
                fault = jnp.where(jnp.abs(e) < TOLERANCE, fault, 1.0)
            p = upper if p is None else dot3(split(p), us)
        s = p * down
        ss = split(s)
        q = dot3(split(images[:, spec(k)]), ss)
        out[:, spec(k)] = q.astype(BF16)
        if k < NB - 1:
            rest = slice((k + 1) * B, N)
            r = dot3(split(s.T), split(gram[spec(k), rest]))
            rs = split(r)
            gram[rest, rest] = gram[rest, rest] - dot3(rs, rs, dot_tn)
            images[:, rest] = images[:, rest] - dot3(split(q), rs)

    @pl.when(jnp.max(fault) > 0.0)
    def _():
        images[...] = start[...].astype(F32)
        for repeat in range(2):
            image = jnp.dot(
                factor[...].astype(F32), images[...], precision=FULL, preferred_element_type=F32
            )
            images[...] = image
            gram[...] = lax.dot_general(
                image, image, (((0,), (0,)), ((), ())), precision=FULL, preferred_element_type=F32
            )
            eliminate(gram, images)
        out[...] = images[...].astype(BF16)


def turn_kernel(mine, theirs, rows, out, bases):
    core = here()[1]
    for k in range(CHIPS):
        bases[core, spec(k % NB), spec(k // NB)] = mine[k, PF:, :]
        bases[1 - core, spec(k % NB), spec(k // NB)] = theirs[k, PF:, :]
    moment = rows[:, STEP : 2 * STEP, :].reshape(N, N)
    half = dot(bases[0], moment).astype(BF16)
    out[...] = dot_nt(half, bases[1]).astype(BF16)


def final_kernel(mine, theirs, turned, rows, square, fresh, moment_out, square_out, update, mom, rot):
    replica, core = here()
    fresh[core] = mine[...]
    fresh[1 - core] = theirs[...]
    left = fresh[0]
    right = fresh[1]
    grad = rows[:, :STEP, :].reshape(N, N)
    projected = dot(grad, right).astype(BF16)
    moment = dot(turned[...], right).astype(BF16)
    gradient_rot = dot_tn(left, projected)
    moment_rot = dot_tn(left, moment)
    new = 0.9 * moment_rot + 0.1 * gradient_rot
    mom[...] = new
    rot[...] = gradient_rot
    squares = rows[:, 2 * STEP :, :].reshape(N, N).astype(F32)
    level = 0.95 * squares + 0.05 * gradient_rot * gradient_rot
    direction = (new / (jnp.sqrt(level) + 1e-08)).astype(BF16)
    returned = dot_nt(direction, right).astype(BF16)
    at = pl.ds(pl.multiple_of(replica * STEP, STEP), STEP)
    moment_out[...] = mom[at, :]
    own = rot[at, :]
    square_out[...] = 0.95 * square[...] + 0.05 * own * own
    update[...] = dot(fresh[0, at, :], returned).astype(BF16)


def shape(dims, dtype):
    return jax.ShapeDtypeStruct(dims, dtype)


def call(kernel, name, out, specs, scratch=(), flops=0):
    return pl.pallas_call(
        kernel,
        name=name,
        out_shape=out,
        in_specs=specs,
        scratch_shapes=list(scratch),
        compiler_params=PARAMS,
        cost_estimate=pl.CostEstimate(flops=flops, bytes_accessed=2**21, transcendentals=0),
    )


def on_device(partials, basis_store, owner_table, grad, exp_avg, exp_avg_sq):
    devices = 2 * CHIPS
    swap = [(i, i ^ 1) for i in range(devices)]
    down = [(i, i - 1) for i in range(1, devices, 2)]
    groups = [list(range(c, devices, 2)) for c in range(2)]

    rows = jnp.concatenate([grad[0], exp_avg[0].astype(BF16), exp_avg_sq[0].astype(BF16)], axis=0)
    rows = lax.all_gather(rows, "dp", axis=0, tiled=False)

    part = partials[0, 0]
    stored = basis_store[0, 0]
    got_basis = lax.ppermute(stored, "dp", down)
    packed = call(pack_kernel, "pack", shape((PACK, B), BF16), [VMEM])(part)
    got = lax.ppermute(packed, "dp", swap)
    payload = call(pair_kernel, "pair", shape((CHIPS, PIECE, B), BF16), [VMEM] * 4)(
        part, got, got_basis, stored
    )
    got = lax.all_to_all(payload, "dp", 0, 0, tiled=True, axis_index_groups=groups)
    payload = call(sum_kernel, "sum", shape((CHIPS, PIECE, B), BF16), [SMEM, VMEM])(owner_table, got)
    whole = lax.all_to_all(payload, "dp", 0, 0, tiled=True, axis_index_groups=groups)
    whole_other = lax.ppermute(whole, "dp", swap)
    mine = call(
        basis_kernel,
        "basis",
        shape((N, N), BF16),
        [VMEM],
        [
            pltpu.VMEM((N, N), BF16),
            pltpu.VMEM((N, N), BF16),
            pltpu.VMEM((PACK, B), BF16),
            pltpu.VMEM((N, N), F32),
            pltpu.VMEM((N, N), F32),
        ],
        flops=0,
    )(whole)
    theirs = lax.ppermute(mine, "dp", swap)
    turned = call(
        turn_kernel, "turn", shape((N, N), BF16), [VMEM] * 3, [pltpu.VMEM((2, N, N), BF16)], flops=0
    )(whole, whole_other, rows)
    fresh, moment_new, square_new, update = call(
        final_kernel,
        "final",
        (
            shape((2, N, N), BF16),
            shape((STEP, N), F32),
            shape((STEP, N), F32),
            shape((STEP, N), BF16),
        ),
        [VMEM] * 5,
        [pltpu.VMEM((N, N), F32), pltpu.VMEM((N, N), F32)],
        flops=0,
    )(mine, theirs, turned, rows, exp_avg_sq[0])
    return fresh[None], moment_new[None], square_new[None], update[None]


def solution(mesh):
    in_specs = (
        P("dp", "fsdp", None, None, None),
        P("dp", "fsdp", None, None, None),
        P(),
        P("fsdp", "dp", None),
        P("fsdp", "dp", None),
        P("fsdp", "dp", None),
    )
    out_specs = (
        P("fsdp", None, None, None),
        P("fsdp", "dp", None),
        P("fsdp", "dp", None),
        P("fsdp", "dp", None),
    )
    return jax.shard_map(
        on_device, mesh=mesh, in_specs=in_specs, out_specs=out_specs, check_vma=False
    )
```
